1024 devices in a mesh: node: 16 (over x, y), local: 64 (over z, core).
Axes of the slice: x: 4, y: 4, z: 32, core: 2. Of those that a mesh axis runs over, the one named last changes fastest.
Arguments:
- grad_out: bfloat16 [8192, 7168], P(('node', 'local')), may hold values from -6 to 6
- inputs: bfloat16 [8192, 7168], P(('node', 'local')), may hold values from -6 to 6
- group_ids: int32 [8192, 4], P(('node', 'local')), may hold values from 0 to 15, all different within a row; in each aligned block of 8 rows (0 to 7, 8 to 15, ...) at most 4 rows name the same one
- pair_code: int32 [8192, 4], P(('node', 'local')), may hold values from 0 to 239
- combine: bfloat16 [8192, 8], P(('node', 'local')), may hold values from 0.19921875 to 1
- w_gate: bfloat16 [1024, 1792, 128], P(('node', 'local')), may hold values from -0.0625 to 0.0625
- w_up: bfloat16 [1024, 1792, 128], P(('node', 'local')), may hold values from -0.0625 to 0.0625
- w_down: bfloat16 [1024, 128, 1792], P(('node', 'local')), may hold values from -0.125 to 0.125
Outputs:
- grad_inputs: bfloat16 [8192, 7168], P(('node', 'local'))
- grad_gate: bfloat16 [1024, 1792, 128], P(('node', 'local'))
- grad_up: bfloat16 [1024, 1792, 128], P(('node', 'local'))
- grad_down: bfloat16 [1024, 128, 1792], P(('node', 'local'))
The draws below stay inside these ranges and needn't reach their ends.
Inputs may be any that keep to these rules, and one draw needn't show every extreme that they name: `group_ids`: each row names 4 different node groups; among the 8 rows of one device no group is named by more than 4 rows.
All inputs are finite; a program needn't handle non-finite values.
Results may differ from the reference program's by a relative error of at most 0.019.
Values may be sent and summed in bfloat16 or wider, within the bound.
A program may use at most 32 MiB of HBM per device.

```python
import math
import jax
import jax.numpy as jnp
import numpy as np
from jax import lax

D = 7168
FF_E = 2048
TOP = 8
GSEL = 4
EXP_GROUP = 16
DQ = 4
CAPE = 4
TOK_DEV = 8
HSH = 16
HID_DEV = 128
FEAT = 1792
SLOTS = 256
TOKENS = 8192
CAPG = 4
N_NODE = 16
N_LOCAL = 64


def plant(drawn, rng, low, top_value):
    spot = [jax.random.randint(jax.random.fold_in(rng, axis), (), 0, length) for axis, length in enumerate(drawn.shape)]
    widest = drawn.shape.index(max(drawn.shape))
    next_to = spot[:widest] + [(spot[widest] + 1) % drawn.shape[widest]] + spot[widest + 1:]
    return drawn.at[tuple(spot)].set(low).at[tuple(next_to)].set(top_value)


def steps_of(key, extent, split, smallest, top_value):
    factor_of = 1.0
    for dim, shards_of in split:
        draws = jax.random.uniform(jax.random.fold_in(jax.random.fold_in(key, 6), dim), (shards_of,), jnp.float32, smallest / len(split), top_value / len(split))
        factor_of = factor_of * jnp.repeat(jnp.exp(draws), extent[dim] // shards_of).reshape((-1,) + (1,) * (len(extent) - 1 - dim))
    return factor_of


def assign_block(rng, own, number, rows, count, top, limit, skew):
    sequence = jax.random.permutation(rng, count)
    crowded, ordinary = load_shares(count, rows * top, limit, skew, True), load_shares(count, rows * top, limit, skew, False)
    places = jnp.arange(count)

    def named(lengths, rotation):
        used = int((lengths > 0).sum())
        fixed = max(1, used // 4)
        shifted = fixed + (places - fixed + rotation * (used - fixed)) % max(1, count - fixed)
        return jnp.zeros((count,), jnp.int32).at[sequence[jnp.where(places < fixed, places, shifted)]].set(jnp.asarray(lengths, jnp.int32))

    lengths = jnp.where(number % 4 == 0, named(crowded, number // 4), named(ordinary, number - number // 4 - 1))
    mixed = jax.random.permutation(jax.random.fold_in(own, 3), count)
    giver, sink = mixed[0:count // 2 * 2:2], mixed[1:count // 2 * 2:2]
    slack = jnp.minimum(lengths[giver] - 1, limit - lengths[sink]) // 2
    slack = jnp.where((giver == sequence[0]) | (sink == sequence[0]) | (lengths[sink] == 0), 0, jnp.maximum(slack, 0))
    shifted = jax.random.randint(jax.random.fold_in(own, 4), (count // 2,), 0, 1 << 20) % (slack + 1)
    lengths = lengths.at[giver].add(-shifted).at[sink].add(shifted)
    members = jnp.searchsorted(jnp.cumsum(lengths), jnp.arange(rows * top), side="right").astype(jnp.int32)
    table = members.reshape(top, rows).T
    table = table[jax.random.permutation(jax.random.fold_in(own, 1), rows)]
    rotation = jax.random.randint(jax.random.fold_in(own, 2), (rows, 1), 0, top)
    return jnp.take_along_axis(table, (jnp.arange(top)[None, :] + rotation) % top, axis=1)


def load_shares(count, total, limit, slope, full):
    weights = [(1 << 20) // math.isqrt(rank ** slope) + 1 for rank in range(1, count + 1)]
    largest = limit if full else min(limit, max(-(-total // count), total * weights[0] // sum(weights)))
    least = 1 if total - largest >= count - 1 else 0
    holding, surplus = [largest] + [least] * (count - 1), total - largest - least * (count - 1)
    while surplus > 0:
        movable = [i for i in range(1, count) if holding[i] < largest] or [i for i in range(1, count) if holding[i] < limit]
        mass, left = sum([weights[i] for i in movable]), surplus
        for i in movable:
            addition = min(limit - holding[i], max(1, left * weights[i] // mass), surplus)
            holding[i] = holding[i] + addition
            surplus = surplus - addition
    return np.array(holding)


def noise(key, dims, deviation, most, pieces=(), kind=jnp.bfloat16):
    result = jax.random.normal(key, dims, jnp.float32) * deviation
    if len(pieces) > 0:
        result = steps_of(key, dims, pieces, -0.22, 0.18) * result
    return jnp.clip(result, min=-most, max=most).astype(kind)


def setup_inputs(seed: int = 0) -> dict:
    arg_keys = jax.random.split(jax.random.key(seed), 9)
    grad_out = noise(arg_keys[0], (TOKENS, D), 1.0, 6.0, ((0, 1024),))
    inputs = noise(arg_keys[1], (TOKENS, D), 1.0, 6.0, ((0, 1024),))
    group_ids_keys = jax.random.split(jax.random.fold_in(arg_keys[2], 1), TOKENS // TOK_DEV)
    group_ids_turns = jax.random.permutation(jax.random.fold_in(arg_keys[2], 3), TOKENS // TOK_DEV)
    group_ids = jax.vmap(lambda own, number: assign_block(jax.random.fold_in(arg_keys[2], 2), own, number, TOK_DEV, N_NODE, GSEL, CAPG, 2))(group_ids_keys, group_ids_turns).reshape((TOKENS, GSEL))
    pair_code = plant(jax.random.randint(arg_keys[3], (TOKENS, GSEL), 0, EXP_GROUP * (EXP_GROUP - 1)), jax.random.fold_in(arg_keys[3], 1), 0, (EXP_GROUP * (EXP_GROUP - 1)) - 1).astype(jnp.int32)
    combine = jnp.clip(0.19921875 + 0.80078125 * jax.random.uniform(arg_keys[4], (TOKENS, TOP), jnp.float32) ** steps_of(arg_keys[4], (TOKENS, TOP), ((0, 1024),), -0.2, 0.2), 0.19921875, 1.0).astype(jnp.bfloat16)
    w_gate = noise(arg_keys[5], (N_NODE * N_LOCAL, FEAT, HID_DEV), D ** -0.5, 0.0625, ((0, 1024),))
    w_up = noise(arg_keys[6], (N_NODE * N_LOCAL, FEAT, HID_DEV), D ** -0.5, 0.0625, ((0, 1024),))
    w_down = noise(arg_keys[7], (N_NODE * N_LOCAL, HID_DEV, FEAT), FF_E ** -0.5, 0.125, ((0, 1024),))
    return {"grad_out": grad_out, "inputs": inputs, "group_ids": group_ids, "pair_code": pair_code, "combine": combine, "w_gate": w_gate, "w_up": w_up, "w_down": w_down}


def expert_choice(group_ids, pair_code):
    first_pick = pair_code // (EXP_GROUP - 1)
    second_pick = (first_pick + 1 + pair_code % (EXP_GROUP - 1)) % EXP_GROUP
    pick_pairs = jnp.stack([first_pick, second_pick], axis=-1)
    chosen = group_ids[:, :, None] * EXP_GROUP + pick_pairs
    return chosen.reshape(group_ids.shape[0], TOP).astype(jnp.int32)


def window_weight(expert_ids, combine, node_count):
    targets = jnp.arange(node_count, dtype=jnp.int32) * EXP_GROUP
    matches = expert_ids[:, :, None] == targets[None, None, :]
    values = jnp.where(matches, combine.astype(jnp.float32)[:, :, None], jnp.float32(0.0))
    return jnp.sum(values, axis=1).astype(jnp.bfloat16)


def to_columns(rows):
    model_width = rows.shape[-1]
    shaped = rows.reshape(N_NODE, N_LOCAL, TOK_DEV, model_width)
    return jnp.transpose(shaped, (1, 0, 2, 3)).reshape(N_LOCAL, N_NODE * TOK_DEV, model_width)


def reference(grad_out, inputs, group_ids, pair_code, combine, w_gate, w_up, w_down):
    highest = lax.Precision.HIGHEST
    expert_ids = expert_choice(group_ids, pair_code)
    window = window_weight(expert_ids, combine, N_NODE)
    column_weight = to_columns(window).astype(jnp.float32)
    is_live = (column_weight > 0).astype(jnp.int32)
    live_rank = jnp.cumsum(is_live, axis=1) - is_live
    slot_index = jnp.arange(CAPE, dtype=jnp.int32)
    onehot = ((is_live[:, None, :, :] == 1) & (live_rank[:, None, :, :] == slot_index[None, :, None, None])).astype(jnp.float32)
    dy_columns = to_columns(grad_out)
    x_columns = to_columns(inputs)

    def one_expert(running, group_index):
        weight_here = lax.dynamic_index_in_dim(column_weight, group_index, 2, keepdims=False)
        chooser = lax.dynamic_index_in_dim(onehot, group_index, 3, keepdims=False)
        scaled = (weight_here[:, :, None] * dy_columns.astype(jnp.float32)).astype(jnp.bfloat16)
        slot_dy = jnp.einsum("lcr,lrd->lcd", chooser, scaled.astype(jnp.float32), precision=highest)
        slot_dy = slot_dy.astype(jnp.bfloat16).reshape(SLOTS, D)
        slot_x = jnp.einsum("lcr,lrd->lcd", chooser, x_columns.astype(jnp.float32), precision=highest)
        slot_x = slot_x.astype(jnp.bfloat16).reshape(SLOTS, D)
        block_start = group_index * N_LOCAL
        gate_blocks = lax.dynamic_slice_in_dim(w_gate, block_start, N_LOCAL, 0)
        up_blocks = lax.dynamic_slice_in_dim(w_up, block_start, N_LOCAL, 0)
        down_blocks = lax.dynamic_slice_in_dim(w_down, block_start, N_LOCAL, 0)
        full_gate = jnp.transpose(gate_blocks.reshape(HSH, DQ, FEAT, HID_DEV), (1, 2, 0, 3)).reshape(D, FF_E)
        full_up = jnp.transpose(up_blocks.reshape(HSH, DQ, FEAT, HID_DEV), (1, 2, 0, 3)).reshape(D, FF_E)
        full_down = jnp.transpose(down_blocks.reshape(HSH, DQ, HID_DEV, FEAT), (0, 2, 1, 3)).reshape(FF_E, D)
        gate_pre = jnp.dot(slot_x, full_gate, preferred_element_type=jnp.float32)
        up_pre = jnp.dot(slot_x, full_up, preferred_element_type=jnp.float32)
        hidden_grad = jnp.dot(slot_dy, full_down.T, preferred_element_type=jnp.float32)
        sigmoid_gate = jax.nn.sigmoid(gate_pre)
        activated = gate_pre * sigmoid_gate
        hidden = (activated * up_pre).astype(jnp.bfloat16)
        delta_up = (hidden_grad * activated).astype(jnp.bfloat16)
        delta_gate = (hidden_grad * up_pre * sigmoid_gate * (1.0 + gate_pre * (1.0 - sigmoid_gate))).astype(jnp.bfloat16)
        down_grad = jnp.dot(hidden.T, slot_dy, preferred_element_type=jnp.float32).astype(jnp.bfloat16)
        gate_grad = jnp.dot(slot_x.T, delta_gate, preferred_element_type=jnp.float32).astype(jnp.bfloat16)
        up_grad = jnp.dot(slot_x.T, delta_up, preferred_element_type=jnp.float32).astype(jnp.bfloat16)
        down_out = jnp.transpose(down_grad.reshape(HSH, HID_DEV, DQ, FEAT), (0, 2, 1, 3)).reshape(N_LOCAL, HID_DEV, FEAT)
        gate_out = jnp.transpose(gate_grad.reshape(DQ, FEAT, HSH, HID_DEV), (2, 0, 1, 3)).reshape(N_LOCAL, FEAT, HID_DEV)
        up_out = jnp.transpose(up_grad.reshape(DQ, FEAT, HSH, HID_DEV), (2, 0, 1, 3)).reshape(N_LOCAL, FEAT, HID_DEV)
        gate_parts = jnp.einsum("sah,dah->sad", delta_gate.astype(jnp.float32).reshape(SLOTS, HSH, HID_DEV), full_gate.astype(jnp.float32).reshape(D, HSH, HID_DEV))
        up_parts = jnp.einsum("sah,dah->sad", delta_up.astype(jnp.float32).reshape(SLOTS, HSH, HID_DEV), full_up.astype(jnp.float32).reshape(D, HSH, HID_DEV))
        shard_parts = (gate_parts + up_parts).astype(jnp.bfloat16)
        relay_sum = jnp.sum(shard_parts.astype(jnp.float32), axis=1).astype(jnp.bfloat16)
        returned = jnp.einsum("lcr,lcd->lrd", chooser, relay_sum.astype(jnp.float32).reshape(N_LOCAL, CAPE, D), precision=highest)
        return running + returned, (gate_out, up_out, down_out)

    start_value = jnp.zeros((N_LOCAL, N_NODE * TOK_DEV, D), jnp.float32)
    accumulated, stacked = lax.scan(one_expert, start_value, jnp.arange(N_NODE, dtype=jnp.int32))
    grad_inputs = jnp.transpose(accumulated.reshape(N_LOCAL, N_NODE, TOK_DEV, D), (1, 0, 2, 3)).reshape(TOKENS, D)
    grad_gate = stacked[0].reshape(N_NODE * N_LOCAL, FEAT, HID_DEV)
    grad_up = stacked[1].reshape(N_NODE * N_LOCAL, FEAT, HID_DEV)
    grad_down = stacked[2].reshape(N_NODE * N_LOCAL, HID_DEV, FEAT)
    return grad_inputs.astype(jnp.bfloat16), grad_gate, grad_up, grad_down
```

```python
import functools
import math

import jax
import jax.numpy as jnp
from jax import lax
from jax.experimental import pallas as pl
from jax.experimental.pallas import tpu as pltpu
from jax.sharding import PartitionSpec as P

EXP_GROUP = 16
DQ = 4
CAPE = 4
TOK = 8
ROWS = DQ * CAPE
LANES = 128
GROUPS = 16
LAG = 1
AHEAD = 4
AG_JUMP = (0, 0, 0, 0)
RS_JUMP = 3
MESH = pl.DeviceIdType.MESH
F32 = jnp.float32
BF16 = jnp.bfloat16


def iota(shape, dim):
    return lax.broadcasted_iota(jnp.int32, shape, dim)


def grid_of(rows, cols):
    return iota((rows, cols), 0), iota((rows, cols), 1)


def one(where):
    return jnp.where(where, 1.0, 0.0).astype(BF16)


def dot(a, b, contract=((1,), (0,))):
    return lax.dot_general(a, b, (contract, ((), ())), preferred_element_type=F32)


LAST = ((1,), (1,))
FIRST = ((0,), (0,))


class Route:
    def __init__(self, far, jump):
        self.far = far
        self.jump = jump if 1 < jump <= far else 0

    def parent(self, i):
        return 0 if i == self.jump else i - 1

    def children(self, p):
        return [i for i in range(1, self.far + 1) if self.parent(i) == p]

    def arrival(self, i):
        return i if not self.jump or i < self.jump else i - self.jump + 2

    def last(self):
        return max(self.arrival(i) for i in range(1, self.far + 1))


def pieces_of(half):
    tiles = half // LANES
    lead = (tiles + 1) // 2
    out = []
    for h in range(2):
        out.append((h, h * half, lead * LANES))
        if tiles > lead:
            out.append((h, h * half + lead * LANES, (tiles - lead) * LANES))
    return out


def kernel(
    nx, ny, nq,
    grad_ref, inp_ref, gid_ref, code_ref, comb_ref, wg_ref, wu_ref, wd_ref,
    fin, gg_ref, gu_ref, gd_ref,
    tok_out, tok, win, wts, packed, cnt, cnts, arrived, xs, dys, wgu,
    mine, part, quad_in, hgrad, hpart, hquad_in, hid, back,
    summed, leaves, relay, allrelay, fin_out,
    tok_send, tok_recv, win_send, win_recv, pack_send, pack_recv, cnt_send, cnt_recv,
    ag_send, ag_recv, mid_send, mid_recv, hid_send, hid_recv,
    rs_send, rs_recv, rel_send, rel_recv, fin_send, fin_recv,
):
    nodes = nx * ny
    feat = wg_ref.shape[0]
    hw = wg_ref.shape[1]
    half = feat // 2
    slots = nodes * ROWS
    to_right = nq // 2
    steps_of = (to_right, nq - 1 - to_right)
    me_n = lax.axis_index("node")
    me_l = lax.axis_index("local")
    quad = lax.div(me_l, DQ)
    b = lax.rem(me_l, DQ)
    my_x, my_y = lax.div(me_n, ny), lax.rem(me_n, ny)

    def quad_at(k):
        return (me_n, lax.rem(quad + (k + nq) % nq, nq) * DQ + b)

    ag_routes = [[Route(far, jump) for far in steps_of] for jump in AG_JUMP]
    rs_routes = [Route(far, RS_JUMP) for far in steps_of]
    apart = {1, nq - 1}
    for route in sum(ag_routes, rs_routes):
        if route.jump:
            apart |= {route.jump, nq - route.jump}
    offsets = [(dx, dy) for dx in range(nx) for dy in range(ny) if dx or dy]
    peers = range(len(offsets))
    mates = range(1, DQ)
    spans = [pl.ds(h * half, half) for h in range(2)]
    started = []

    def go(c):
        c.start()
        started.append(c)

    def node_at(dx, dy):
        return lax.rem(my_x + dx, nx) * ny + lax.rem(my_y + dy, ny)

    def node_to(k):
        dx, dy = offsets[k]
        return node_at(dx, dy)

    def node_from(k):
        dx, dy = offsets[k]
        return node_at(nx - dx, ny - dy)

    def mate(d):
        return lax.bitwise_xor(b, d)

    def in_quad(d):
        return (me_n, quad * DQ + mate(d))

    def copy(src, dst, send, recv, device):
        return pltpu.make_async_remote_copy(
            src_ref=src, dst_ref=dst, send_sem=send, recv_sem=recv,
            device_id=device, device_id_type=MESH,
        )

    barrier = pltpu.get_barrier_semaphore()
    greet = [(node_to(k), me_l) for k in peers] + [in_quad(d) for d in mates]
    greet += [quad_at(k) for k in sorted(apart)]
    for device in greet:
        pl.semaphore_signal(barrier, inc=1, device_id=device, device_id_type=MESH)

    for q in range(DQ):
        for h in range(2):
            at = slice(q * feat + h * half, q * feat + (h + 1) * half)
            tok_out[h, q] = jnp.concatenate(
                [inp_ref[:, at].astype(F32), grad_ref[:, at].astype(F32)], axis=0
            ).astype(BF16)
    chosen, top = gid_ref.shape[0], comb_ref.shape[1]
    code = code_ref[...]
    first = jnp.zeros_like(code)
    for m in range(1, EXP_GROUP):
        first = first + jnp.where(code >= m * (EXP_GROUP - 1), 1, 0)
    second = first + 1 + (code - (EXP_GROUP - 1) * first)
    second = jnp.where(second >= EXP_GROUP, second - EXP_GROUP, second)
    row, col = grid_of(chosen, top)
    comb = comb_ref[...]
    weight = jnp.where(first == 0, dot(one(col == 2 * row), comb, LAST), 0.0)
    weight = weight + jnp.where(second == 0, dot(one(col == 2 * row + 1), comb, LAST), 0.0)
    window = jnp.zeros((GROUPS, TOK), F32)
    for k in range(chosen):
        named = iota((GROUPS, TOK), 0) == gid_ref[k:k + 1, :]
        window = window + jnp.where(named, weight[k:k + 1, :], 0.0)
    row, col = grid_of(TOK, LANES)
    win[...] = dot(window.astype(BF16), one(row == col))

    pl.semaphore_wait(barrier, len(greet))

    def tok_copy(d, h, slot):
        return copy(
            tok_out.at[h, mate(d)], tok.at[h, slot], tok_send.at[h, d], tok_recv.at[h, d],
            in_quad(d),
        )

    def win_copy(d, slot):
        return copy(win, wts.at[slot], win_send.at[d], win_recv.at[d], in_quad(d))

    for d in mates:
        go(win_copy(d, b))
    for h in range(2):
        for d in mates:
            go(tok_copy(d, h, b))
        tok[h, b] = tok_out[h, b]
    wts[b] = win[...]

    cols = 2 * DQ * TOK
    row, col = grid_of(cols, cols)
    below = one((row >> 3 == col >> 3) & (row < col))
    row, col = grid_of(cols, slots)
    tally = one((((row >> 3) & 1) == 0) & (row >> 4 == (col >> 2) & 3) & (col >> 4 == me_n))
    row, col = grid_of(slots, GROUPS)
    of_group = one(row >> 4 == col)
    row, col = grid_of(GROUPS, slots)
    group_of = one(row == col >> 4)
    row, col = grid_of(slots, slots)
    before = one((row >> 4 < col >> 4) & ((row & 15) == (col & 15)))
    row, col = grid_of(slots, cols)
    own_base = one((row >> 4 == me_n) & ((row & 3) == 0) & (((row >> 2) & 3) == col >> 4))
    wgu[:, 0:hw] = wg_ref[...]
    wgu[:, hw:2 * hw] = wu_ref[...]

    for d in mates:
        win_copy(d, mate(d)).wait_recv()
    weights = jnp.zeros((GROUPS, cols), F32)
    row, col = grid_of(LANES, cols)
    for j in range(DQ):
        weights = weights + dot(wts[j].astype(BF16), one((row == (col & 7)) & (col >> 4 == j)))
    live = one(weights > 0)
    ranks = dot(live, below)
    cnt[...] = dot(live, tally).astype(BF16)

    def cnt_copy(k, slot):
        return copy(cnt, cnts.at[slot], cnt_send.at[k], cnt_recv.at[k], (node_to(k), me_l))

    def pack_copy(c, k, slot):
        return copy(
            packed.at[c, node_to(k)], arrived.at[c, slot], pack_send.at[c, k], pack_recv.at[c, k],
            (node_to(k), me_l),
        )

    w_at = dot(of_group, weights.astype(BF16))
    r_at = dot(of_group, ranks.astype(BF16))
    row, col = grid_of(slots, cols)
    fits = ((row >> 2) & 3) == col >> 4
    fits = fits & (r_at == (row & 3).astype(F32)) & (w_at > 0)
    is_grad = ((col >> 3) & 1) == 1
    picks = [
        one(fits & jnp.logical_not(is_grad)),
        jnp.where(fits & is_grad, w_at, 0.0).astype(BF16),
    ]

    def pack(c):
        a, h = c // 2, c % 2
        rows = dot(picks[a], tok[h].reshape(cols, half))
        packed[c] = rows.astype(BF16).reshape(nodes, ROWS, half)
        arrived[c, me_n] = packed[c, me_n]

    def pack_go(c):
        for k in peers:
            go(pack_copy(c, k, me_n))

    for d in mates:
        tok_copy(d, 0, mate(d)).wait_recv()
    pack(0)
    pack_go(0)
    for k in peers:
        go(cnt_copy(k, me_n))
    cnts[me_n] = cnt[...]
    for d in mates:
        tok_copy(d, 1, mate(d)).wait_recv()
    pack(1)
    for c in range(1, AHEAD):
        if c > 1:
            pack(c)
        pack_go(c)
    for c in range(max(2, AHEAD), 4):
        pack(c)

    for k in peers:
        cnt_copy(k, node_from(k)).wait_recv()
    counts = jnp.zeros((GROUPS, slots), F32)
    for m in range(nodes):
        counts = counts + cnts[m].astype(F32)
    begin = dot(counts.astype(BF16), before).astype(BF16)
    row, col = grid_of(ROWS, GROUPS)
    start = dot(one(col == me_n), begin)
    row, col = grid_of(ROWS, slots)
    merge = one(
        (row >> 2 == (col >> 2) & 3) & ((row & 3).astype(F32) == start + (col & 3).astype(F32))
    )
    place = jnp.where(weights > 0, ranks + dot(begin, own_base), 255.0)
    place = dot(place.astype(BF16), group_of, FIRST)
    row, col = grid_of(cols, slots)
    stands = (row >> 4 == (col >> 2) & 3) & (place == (col & 3).astype(F32))
    collect = [one(stands & (((row >> 3) & 1) == h)) for h in range(2)]

    rings = (xs, dys)

    def block(c, i):
        return rings[c // 2].at[pl.ds(i * ROWS, ROWS), spans[c % 2]]

    def place_of(way, i):
        return i if way == 0 else (nq - i) % nq

    def ag_copy(c, way, i):
        p = ag_routes[c][way].parent(i)
        src, dst = place_of(way, p), place_of(way, i)
        return copy(
            block(c, src), block(c, dst), ag_send.at[c, dst], ag_recv.at[c, dst],
            quad_at(i - p if way == 0 else p - i),
        )

    def ag_wait(c, way, i):
        dst = place_of(way, i)
        copy(
            block(c, dst), block(c, dst), ag_send.at[c, dst], ag_recv.at[c, dst], quad_at(1)
        ).wait_recv()

    share = nq * ROWS // DQ

    def rows_at(ref, owner, at, width):
        return ref.at[pl.ds(pl.multiple_of(owner * share, share), share), pl.ds(at, width)]

    def own_rows(ref):
        return ref[pl.ds(pl.multiple_of(b * share, share), share), :]

    def mid_copy(d):
        return copy(
            rows_at(part, mate(d), 0, 2 * hw), quad_in.at[d - 1],
            mid_send.at[0, d], mid_recv.at[0, d], in_quad(d),
        )

    def hgrad_copy(d):
        return copy(
            rows_at(hpart, mate(d), 0, hw), hquad_in.at[d - 1],
            mid_send.at[1, d], mid_recv.at[1, d], in_quad(d),
        )

    whole = set()

    def after_chunk(c):
        span = slice((c % 2) * half, (c % 2 + 1) * half)
        whole.add(c)
        a = c // 2
        if a == 0:
            total = dot(xs[:, span], wgu[span, :])
        else:
            total = dot(dys[:, span], wd_ref[:, span], LAST)
        both = {2 * a, 2 * a + 1} <= whole
        keep, send, move = ((mine, part, mid_copy), (hgrad, hpart, hgrad_copy))[a]
        if both:
            total = keep[...] + total
            send[...] = total.astype(BF16)
            for d in mates:
                go(move(d))
        keep[...] = total

    last = [max(route.last() for route in routes) for routes in ag_routes]
    for turn in range(max(last[c] + LAG * c for c in range(4)) + 1):
        for c in range(4):
            step = turn - LAG * c
            if step == 0:
                for k in peers:
                    pack_copy(c, k, node_from(k)).wait_recv()
                merged = dot(merge, arrived[c].reshape(slots, half)).astype(BF16)
                rings[c // 2][0:ROWS, (c % 2) * half:(c % 2 + 1) * half] = merged
                for way in range(2):
                    for i in reversed(ag_routes[c][way].children(0)):
                        go(ag_copy(c, way, i))
                if c + AHEAD < 4:
                    pack_go(c + AHEAD)
            for way in range(2):
                route = ag_routes[c][way]
                for i in range(route.far, 0, -1):
                    if route.arrival(i) == step:
                        ag_wait(c, way, i)
                        for j in route.children(i):
                            go(ag_copy(c, way, j))
            if step == last[c]:
                after_chunk(c)

    total = own_rows(mine)
    for d in mates:
        mid_copy(d).wait_recv()
        total = total + quad_in[d - 1].astype(F32)
    gate_pre, up_pre = total[:, :hw], total[:, hw:]
    sigmoid_gate = 1.0 / (1.0 + jnp.exp(-gate_pre))
    activated = gate_pre * sigmoid_gate
    slope = up_pre * sigmoid_gate * (1.0 + gate_pre * (1.0 - sigmoid_gate))
    hidden_grad = own_rows(hgrad)
    for d in mates:
        hgrad_copy(d).wait_recv()
        hidden_grad = hidden_grad + hquad_in[d - 1].astype(F32)
    hid[pl.ds(pl.multiple_of(b * share, share), share), :] = jnp.concatenate(
        [hidden_grad * slope, hidden_grad * activated, activated * up_pre], axis=1
    ).astype(BF16)

    def hid_copy(d, owner, i):
        at, width = ((0, 2 * hw), (2 * hw, hw))[i]
        return copy(
            rows_at(hid, b, at, width), rows_at(hid, owner, at, width),
            hid_send.at[i, d], hid_recv.at[i, d], in_quad(d),
        )

    for i in range(2):
        for d in mates:
            go(hid_copy(d, b, i))
    for d in mates:
        hid_copy(d, mate(d), 0).wait_recv()
    deltas = hid[:, 0:2 * hw]
    back[...] = dot(deltas, wgu[...], LAST)

    pieces = pieces_of(half)

    def rs_copy(way, i, p):
        route = rs_routes[way]
        _, at, width = pieces[p]
        span = pl.ds(at, width)
        src = summed.at[way, i + 1, :, span] if route.children(i) else leaf(way, i).at[:, span]
        k = i - route.parent(i)
        return copy(
            src, summed.at[way, i, :, span], rs_send.at[way, i - 1, p], rs_recv.at[way, i - 1, p],
            quad_at(-k if way == 0 else k),
        )

    def leaf(way, i):
        return leaves.at[way, 0 if i == rs_routes[way].far else 1]

    def own_block(way, i, span):
        at = place_of(way, i) * ROWS
        return back[at:at + ROWS, span]

    for step in range(to_right):
        for chain in range(2):
            for p, (_, at, width) in enumerate(pieces):
                span = slice(at, at + width)
                for way in range(2):
                    route = rs_routes[way]
                    i = (route.jump - 1 if chain else route.far) - step
                    if i < (1 if chain else max(route.jump, 1)):
                        continue
                    own = own_block(way, i, span)
                    if step == 0:
                        leaves[way, chain, :, span] = own.astype(BF16)
                    else:
                        rs_copy(way, i + 1, p).wait_recv()
                        summed[way, i + 1, :, span] = (
                            summed[way, i + 1, :, span].astype(F32) + own
                        ).astype(BF16)
                    go(rs_copy(way, i, p))

    def rel_copy(h, k, slot):
        return copy(
            relay.at[h], allrelay.at[h, slot], rel_send.at[h, k], rel_recv.at[h, k],
            (node_to(k), me_l),
        )

    for p, (h, at, width) in enumerate(pieces):
        span = slice(at, at + width)
        acc = back[0:ROWS, span]
        for way in (1, 0):
            for i in rs_routes[way].children(0):
                rs_copy(way, i, p).wait_recv()
                acc = acc + summed[way, i, :, span].astype(F32)
        relay[h, :, at - h * half:at - h * half + width] = acc.astype(BF16)
        if at + width == (h + 1) * half:
            for k in peers:
                go(rel_copy(h, k, me_n))

    allrelay[0, me_n] = relay[0]
    allrelay[1, me_n] = relay[1]
    grads = dot(xs[...], deltas, FIRST)
    gg_ref[...] = grads[:, :hw].astype(BF16)
    gu_ref[...] = grads[:, hw:].astype(BF16)
    for d in mates:
        hid_copy(d, mate(d), 1).wait_recv()
    gd_ref[...] = dot(hid[:, 2 * hw:3 * hw], dys[...], FIRST).astype(BF16)

    sums = jnp.zeros((cols, half), F32)
    for h in range(2):
        for k in peers:
            rel_copy(h, k, node_from(k)).wait_recv()
        sums = sums + dot(collect[h], allrelay[h].reshape(slots, half))
    fin_out[...] = sums.astype(BF16).reshape(DQ, 2 * TOK, half)

    def fin_copy(d, slot):
        return copy(
            fin_out.at[mate(d)], fin.at[slot], fin_send.at[d], fin_recv.at[d], in_quad(d)
        )

    for d in mates:
        go(fin_copy(d, b))
    fin[b] = fin_out[b]
    for d in mates:
        fin_copy(d, mate(d)).wait_recv()
    for c in started:
        c.wait_send()


def hand_on(fin, gg, gu, gd, gi_ref, gg_ref, gu_ref, gd_ref, gg_mid, gu_mid, gd_mid, sem):
    moves = ((gg, gg_mid, gg_ref), (gu, gu_mid, gu_ref), (gd, gd_mid, gd_ref))
    loads = [pltpu.make_async_copy(m[0], m[1], sem.at[0, i]) for i, m in enumerate(moves)]
    stores = [pltpu.make_async_copy(m[1], m[2], sem.at[1, i]) for i, m in enumerate(moves)]
    for c in loads:
        c.start()
    half = fin.shape[2]
    for q in range(DQ):
        got = fin[q].astype(F32)
        for h in range(2):
            at = (2 * q + h) * half
            gi_ref[:, at:at + half] = got[h * TOK:(h + 1) * TOK].astype(BF16)
    for load, store in zip(loads, stores):
        load.wait()
        store.start()
    for c in stores:
        c.wait()


def on_device(shape, grad_out, inputs, group_ids, pair_code, combine, w_gate, w_up, w_down):
    nodes, locals_ = shape
    nx = math.isqrt(nodes)
    ny = nodes // nx
    nq = locals_ // DQ
    feat, hw = w_gate.shape[1:]
    half = feat // 2
    width = grad_out.shape[1]
    ring = nq * ROWS
    slots = nodes * ROWS
    to_right = nq // 2
    pieces = len(pieces_of(half))
    dma = pltpu.SemaphoreType.DMA
    peers = nodes - 1
    operands = (
        grad_out, inputs, group_ids.T, pair_code.T, combine, w_gate[0], w_up[0], w_down[0]
    )
    outs = ((DQ, 2 * TOK, half), (feat, hw), (feat, hw), (hw, feat))

    def whole(dims):
        return pl.BlockSpec(dims, lambda i: (0,) * len(dims))

    hbm = pl.BlockSpec(memory_space=pl.ANY)
    results = pl.pallas_call(
        functools.partial(kernel, nx, ny, nq),
        grid=(1,),
        out_shape=tuple(jax.ShapeDtypeStruct(dims, BF16) for dims in outs),
        in_specs=[whole(o.shape) for o in operands],
        out_specs=tuple(whole(dims) for dims in outs),
        scratch_shapes=[
            pltpu.VMEM((2, DQ, 2 * TOK, half), BF16),
            pltpu.VMEM((2, DQ, 2 * TOK, half), BF16),
            pltpu.VMEM((GROUPS, LANES), F32),
            pltpu.VMEM((DQ, GROUPS, LANES), F32),
            pltpu.VMEM((4, nodes, ROWS, half), BF16),
            pltpu.VMEM((GROUPS, slots), BF16),
            pltpu.VMEM((nodes, GROUPS, slots), BF16),
            pltpu.VMEM((4, nodes, ROWS, half), BF16),
            pltpu.VMEM((ring, feat), BF16),
            pltpu.VMEM((ring, feat), BF16),
            pltpu.VMEM((feat, 2 * hw), BF16),
            pltpu.VMEM((ring, 2 * hw), F32),
            pltpu.VMEM((ring, 2 * hw), BF16),
            pltpu.VMEM((DQ - 1, ring // DQ, 2 * hw), BF16),
            pltpu.VMEM((ring, hw), F32),
            pltpu.VMEM((ring, hw), BF16),
            pltpu.VMEM((DQ - 1, ring // DQ, hw), BF16),
            pltpu.VMEM((ring, 3 * hw), BF16),
            pltpu.VMEM((ring, feat), F32),
            pltpu.VMEM((2, to_right + 1, ROWS, feat), BF16),
            pltpu.VMEM((2, 2, ROWS, feat), BF16),
            pltpu.VMEM((2, ROWS, half), BF16),
            pltpu.VMEM((2, nodes, ROWS, half), BF16),
            pltpu.VMEM((DQ, 2 * TOK, half), BF16),
            dma((2, DQ)), dma((2, DQ)), dma((DQ,)), dma((DQ,)),
            dma((4, peers)), dma((4, peers)), dma((peers,)), dma((peers,)),
            dma((4, nq)), dma((4, nq)),
            dma((2, DQ)), dma((2, DQ)), dma((2, DQ)), dma((2, DQ)),
            dma((2, to_right, pieces)), dma((2, to_right, pieces)),
            dma((2, peers)), dma((2, peers)), dma((DQ,)), dma((DQ,)),
        ],
        compiler_params=pltpu.CompilerParams(
            collective_id=0, has_side_effects=True, vmem_limit_bytes=56 * 1024 * 1024
        ),
    )(*operands)
    gi, gg, gu, gd = pl.pallas_call(
        hand_on,
        grid=(1,),
        out_shape=tuple(
            jax.ShapeDtypeStruct(dims, BF16) for dims in ((TOK, width),) + outs[1:]
        ),
        in_specs=[whole(outs[0]), hbm, hbm, hbm],
        out_specs=(whole((TOK, width)), hbm, hbm, hbm),
        scratch_shapes=[pltpu.VMEM(dims, BF16) for dims in outs[1:]] + [dma((2, 3))],
        compiler_params=pltpu.CompilerParams(vmem_limit_bytes=56 * 1024 * 1024),
    )(*results)
    return gi, gg[None], gu[None], gd[None]


def solution(mesh):
    rows = P(("node", "local"), None)
    blocks = P(("node", "local"), None, None)
    shape = (mesh.shape["node"], mesh.shape["local"])
    return jax.shard_map(
        functools.partial(on_device, shape),
        mesh=mesh,
        in_specs=(rows,) * 5 + (blocks,) * 3,
        out_specs=(rows,) + (blocks,) * 3,
        check_vma=False,
    )
```

```python
import functools
import math

import jax
import jax.numpy as jnp
from jax import lax
from jax.experimental import pallas as pl
from jax.experimental.pallas import tpu as pltpu
from jax.sharding import PartitionSpec as P

EXP_GROUP = 16
DQ = 4
CAPE = 4
TOK = 8
ROWS = DQ * CAPE
LANES = 128
GROUPS = 16
START = (0, 0, 0, 0)
AG_JUMP = (0, 0, 0, 0)
SPLIT = 1
RS_JUMP = 3
MESH = pl.DeviceIdType.MESH
F32 = jnp.float32
BF16 = jnp.bfloat16


def iota(shape, dim):
    return lax.broadcasted_iota(jnp.int32, shape, dim)


def grid_of(rows, cols):
    return iota((rows, cols), 0), iota((rows, cols), 1)


def one(where):
    return jnp.where(where, 1.0, 0.0).astype(BF16)


def dot(a, b, contract=((1,), (0,))):
    return lax.dot_general(a, b, (contract, ((), ())), preferred_element_type=F32)


LAST = ((1,), (1,))
FIRST = ((0,), (0,))


class Route:
    def __init__(self, far, jump):
        self.far = far
        self.jump = jump if 1 < jump <= far else 0

    def parent(self, i):
        return 0 if i == self.jump else i - 1

    def children(self, p):
        return [i for i in range(1, self.far + 1) if self.parent(i) == p]

    def arrival(self, i):
        return i if not self.jump or i < self.jump else i - self.jump + 2

    def last(self):
        return max(self.arrival(i) for i in range(1, self.far + 1))


def pieces_of(half):
    tiles = half // LANES
    lead = (tiles + 1) // 2 if SPLIT else tiles
    out = []
    for h in range(2):
        out.append((h, h * half, lead * LANES))
        if tiles > lead:
            out.append((h, h * half + lead * LANES, (tiles - lead) * LANES))
    return out


def kernel(
    nx, ny, nq,
    grad_ref, inp_ref, gid_ref, code_ref, comb_ref, wg_ref, wu_ref, wd_ref,
    fin, gg_ref, gu_ref, gd_ref,
    tok_out, tok, win, wts, packed, cnt, cnts, arrived, turned, landed, xs, dys, wgu,
    mine, part, core_in, chip_out, chip_in, hid, back,
    summed, leaves, relay, allrelay, fin_out,
    tok_send, tok_recv, win_send, win_recv, along_send, along_recv, across_send, across_recv, cnt_send, cnt_recv,
    ag_send, ag_recv, mid_send, mid_recv,
    rs_send, rs_recv, rel_send, rel_recv, fin_send, fin_recv,
):
    nodes = nx * ny
    feat = wg_ref.shape[0]
    hw = wg_ref.shape[1]
    half = feat // 2
    slots = nodes * ROWS
    to_right = nq // 2
    steps_of = (to_right, nq - 1 - to_right)
    me_n = lax.axis_index("node")
    me_l = lax.axis_index("local")
    quad = lax.div(me_l, DQ)
    b = lax.rem(me_l, DQ)
    my_x, my_y = lax.div(me_n, ny), lax.rem(me_n, ny)

    def quad_at(k):
        return (me_n, lax.rem(quad + (k + nq) % nq, nq) * DQ + b)

    ag_routes = [[Route(far, jump) for far in steps_of] for jump in AG_JUMP]
    rs_routes = [Route(far, RS_JUMP) for far in steps_of]
    apart = {1, nq - 1}
    for route in sum(ag_routes, rs_routes):
        if route.jump:
            apart |= {route.jump, nq - route.jump}
    offsets = [(dx, dy) for dx in range(nx) for dy in range(ny) if dx or dy]
    peers = range(len(offsets))
    mates = range(1, DQ)
    spans = [pl.ds(h * half, half) for h in range(2)]
    started = []

    def go(c):
        c.start()
        started.append(c)

    def node_at(dx, dy):
        return lax.rem(my_x + dx, nx) * ny + lax.rem(my_y + dy, ny)

    def node_to(k):
        dx, dy = offsets[k]
        return node_at(dx, dy)

    def node_from(k):
        dx, dy = offsets[k]
        return node_at(nx - dx, ny - dy)

    def mate(d):
        return lax.bitwise_xor(b, d)

    def in_quad(d):
        return (me_n, quad * DQ + mate(d))

    def copy(src, dst, send, recv, device):
        return pltpu.make_async_remote_copy(
            src_ref=src, dst_ref=dst, send_sem=send, recv_sem=recv,
            device_id=device, device_id_type=MESH,
        )

    barrier = pltpu.get_barrier_semaphore()
    greet = [(node_to(k), me_l) for k in peers] + [in_quad(d) for d in mates]
    greet += [quad_at(k) for k in sorted(apart)]
    for device in greet:
        pl.semaphore_signal(barrier, inc=1, device_id=device, device_id_type=MESH)

    for q in range(DQ):
        for h in range(2):
            at = slice(q * feat + h * half, q * feat + (h + 1) * half)
            tok_out[h, q] = jnp.concatenate(
                [inp_ref[:, at].astype(F32), grad_ref[:, at].astype(F32)], axis=0
            ).astype(BF16)
    chosen, top = gid_ref.shape[0], comb_ref.shape[1]
    code = code_ref[...]
    first = jnp.zeros_like(code)
    for m in range(1, EXP_GROUP):
        first = first + jnp.where(code >= m * (EXP_GROUP - 1), 1, 0)
    second = first + 1 + (code - (EXP_GROUP - 1) * first)
    second = jnp.where(second >= EXP_GROUP, second - EXP_GROUP, second)
    row, col = grid_of(chosen, top)
    comb = comb_ref[...]
    weight = jnp.where(first == 0, dot(one(col == 2 * row), comb, LAST), 0.0)
    weight = weight + jnp.where(second == 0, dot(one(col == 2 * row + 1), comb, LAST), 0.0)
    window = jnp.zeros((GROUPS, TOK), F32)
    for k in range(chosen):
        named = iota((GROUPS, TOK), 0) == gid_ref[k:k + 1, :]
        window = window + jnp.where(named, weight[k:k + 1, :], 0.0)
    row, col = grid_of(TOK, LANES)
    win[...] = dot(window.astype(BF16), one(row == col))

    pl.semaphore_wait(barrier, len(greet))

    def tok_copy(d, h, slot):
        return copy(
            tok_out.at[h, mate(d)], tok.at[h, slot], tok_send.at[h, d], tok_recv.at[h, d],
            in_quad(d),
        )

    def win_copy(d, slot):
        return copy(win, wts.at[slot], win_send.at[d], win_recv.at[d], in_quad(d))

    for d in mates:
        go(win_copy(d, b))
    for h in range(2):
        for d in mates:
            go(tok_copy(d, h, b))
        tok[h, b] = tok_out[h, b]
    wts[b] = win[...]

    cols = 2 * DQ * TOK
    row, col = grid_of(cols, cols)
    below = one((row >> 3 == col >> 3) & (row < col))
    row, col = grid_of(cols, slots)
    tally = one((((row >> 3) & 1) == 0) & (row >> 4 == (col >> 2) & 3) & (col >> 4 == me_n))
    fold = nx.bit_length() - 1

    def group_at(order, u):
        return u if order == 0 else ((u & (nx - 1)) << fold) + (u >> fold)

    row, col = grid_of(slots, GROUPS)
    of_group = [one(group_at(order, row >> 4) == col) for order in range(2)]
    row, col = grid_of(GROUPS, slots)
    group_of = one(row == col >> 4)
    row, col = grid_of(slots, slots)
    before = one((row >> 4 < col >> 4) & ((row & 15) == (col & 15)))
    row, col = grid_of(slots, cols)
    own_base = one((row >> 4 == me_n) & ((row & 3) == 0) & (((row >> 2) & 3) == col >> 4))
    wgu[:, 0:hw] = wg_ref[...]
    wgu[:, hw:2 * hw] = wu_ref[...]

    for d in mates:
        win_copy(d, mate(d)).wait_recv()
    weights = jnp.zeros((GROUPS, cols), F32)
    row, col = grid_of(LANES, cols)
    for j in range(DQ):
        weights = weights + dot(wts[j].astype(BF16), one((row == (col & 7)) & (col >> 4 == j)))
    live = one(weights > 0)
    ranks = dot(live, below)
    cnt[...] = dot(live, tally).astype(BF16)

    def cnt_copy(k, slot):
        return copy(cnt, cnts.at[slot], cnt_send.at[k], cnt_recv.at[k], (node_to(k), me_l))

    at_xy = (my_x, my_y)

    def node_on(axis, t):
        return t * ny + my_y if axis == 0 else my_x * ny + t

    def along_copy(c, k, slot):
        axis = c % 2
        t = lax.rem(at_xy[axis] + k, nx)
        return copy(
            packed.at[c, pl.ds(t * nx, nx)], arrived.at[c, slot],
            along_send.at[c, k], along_recv.at[c, k], (node_on(axis, t), me_l),
        )

    def across_copy(c, k, slot):
        axis = 1 - c % 2
        t = lax.rem(at_xy[axis] + k, nx)
        return copy(
            turned.at[c, t], landed.at[c, slot],
            across_send.at[c, k], across_recv.at[c, k], (node_on(axis, t), me_l),
        )

    picks = []
    row, col = grid_of(slots, cols)
    is_grad = ((col >> 3) & 1) == 1
    for order in range(2):
        w_at = dot(of_group[order], weights.astype(BF16))
        r_at = dot(of_group[order], ranks.astype(BF16))
        fits = ((row >> 2) & 3) == col >> 4
        fits = fits & (r_at == (row & 3).astype(F32)) & (w_at > 0)
        picks.append((
            one(fits & jnp.logical_not(is_grad)),
            jnp.where(fits & is_grad, w_at, 0.0).astype(BF16),
        ))

    def pack(c):
        a, h = c // 2, c % 2
        mine_at = at_xy[c % 2]
        rows = dot(picks[c % 2][a], tok[h].reshape(cols, half))
        packed[c] = rows.astype(BF16).reshape(nodes, ROWS, half)
        for k in range(1, nx):
            go(along_copy(c, k, mine_at))
        arrived[c, mine_at] = packed[c, pl.ds(mine_at * nx, nx)]

    for d in mates:
        tok_copy(d, 0, mate(d)).wait_recv()
    pack(0)
    for k in peers:
        go(cnt_copy(k, me_n))
    cnts[me_n] = cnt[...]
    for d in mates:
        tok_copy(d, 1, mate(d)).wait_recv()
    for c in range(1, 4):
        pack(c)

    for k in peers:
        cnt_copy(k, node_from(k)).wait_recv()
    counts = jnp.zeros((GROUPS, slots), F32)
    for m in range(nodes):
        counts = counts + cnts[m].astype(F32)
    begin = dot(counts.astype(BF16), before).astype(BF16)
    line = nx * ROWS
    merges = []
    for order in range(2):
        row, col = grid_of(line, GROUPS)
        group = my_x * ny + (row >> 4) if order == 0 else (row >> 4) * ny + my_y
        start = dot(one(group == col), begin).astype(BF16)
        row, col = grid_of(slots, slots)
        source = node_on(order, col >> (4 + fold))
        start = dot(
            start,
            one((row >> 4 == source) & ((row & 3) == 0) & ((row >> 2) & 3 == (col >> 2) & 3)),
        )
        row, col = grid_of(line, slots)
        same = (row >> 4 == (col >> 4) & (nx - 1)) & ((row >> 2) & 3 == (col >> 2) & 3)
        merges.append(one(same & ((row & 3).astype(F32) == start + (col & 3).astype(F32))))
    place = jnp.where(weights > 0, ranks + dot(begin, own_base), 255.0)
    place = dot(place.astype(BF16), group_of, FIRST)
    row, col = grid_of(cols, slots)
    stands = (row >> 4 == (col >> 2) & 3) & (place == (col & 3).astype(F32))
    collect = [one(stands & (((row >> 3) & 1) == h)) for h in range(2)]

    def turn_off(c):
        axis = c % 2
        for k in range(1, nx):
            along_copy(c, k, lax.rem(at_xy[axis] + nx - k, nx)).wait_recv()
        rows = dot(merges[axis], arrived[c].reshape(slots, half))
        turned[c] = rows.astype(BF16).reshape(nx, ROWS, half)
        here = at_xy[1 - axis]
        for k in range(1, nx):
            go(across_copy(c, k, here))
        landed[c, here] = turned[c, here]

    def land(c):
        here = at_xy[1 - c % 2]
        for k in range(1, nx):
            across_copy(c, k, lax.rem(here + nx - k, nx)).wait_recv()
        total = landed[c, 0].astype(F32)
        for k in range(1, nx):
            total = total + landed[c, k].astype(F32)
        rings[c // 2][0:ROWS, (c % 2) * half:(c % 2 + 1) * half] = total.astype(BF16)

    for c in range(4):
        if START[c] == 0:
            turn_off(c)

    rings = (xs, dys)

    def block(c, i):
        return rings[c // 2].at[pl.ds(i * ROWS, ROWS), spans[c % 2]]

    def place_of(way, i):
        return i if way == 0 else (nq - i) % nq

    def ag_copy(c, way, i):
        p = ag_routes[c][way].parent(i)
        src, dst = place_of(way, p), place_of(way, i)
        return copy(
            block(c, src), block(c, dst), ag_send.at[c, dst], ag_recv.at[c, dst],
            quad_at(i - p if way == 0 else p - i),
        )

    def ag_wait(c, way, i):
        dst = place_of(way, i)
        copy(
            block(c, dst), block(c, dst), ag_send.at[c, dst], ag_recv.at[c, dst], quad_at(1)
        ).wait_recv()

    whole = set()

    def after_chunk(c):
        span = slice((c % 2) * half, (c % 2 + 1) * half)
        if c // 2 == 0:
            total, at = dot(xs[:, span], wgu[span, :]), slice(0, 2 * hw)
        else:
            total, at = dot(dys[:, span], wd_ref[:, span], LAST), slice(2 * hw, 3 * hw)
        if c ^ 1 in whole:
            total = mine[:, at] + total
        mine[:, at] = total
        whole.add(c)

    last = [max(route.last() for route in routes) for routes in ag_routes]
    for turn in range(max(last[c] + START[c] for c in range(4)) + 1):
        for c in range(4):
            step = turn - START[c]
            if step == 0:
                land(c)
                for way in range(2):
                    for i in reversed(ag_routes[c][way].children(0)):
                        go(ag_copy(c, way, i))
            for way in range(2):
                route = ag_routes[c][way]
                for i in range(route.far, 0, -1):
                    if route.arrival(i) == step:
                        ag_wait(c, way, i)
                        for j in route.children(i):
                            go(ag_copy(c, way, j))
            if step == last[c]:
                after_chunk(c)
        for c in range(4):
            if START[c] == turn + 1:
                turn_off(c)

    core = lax.bitwise_and(b, 1)
    some = nq * ROWS // 2

    def rows_of(ref, owner):
        return ref.at[pl.ds(pl.multiple_of(owner * some, some), some)]

    def core_copy():
        return copy(part, core_in, mid_send.at[0], mid_recv.at[0], in_quad(1))

    def chip_copy():
        return copy(chip_out, rows_of(chip_in, core), mid_send.at[1], mid_recv.at[1], in_quad(2))

    def half_copy(owner):
        rows = rows_of(chip_in, owner)
        return copy(rows, rows, mid_send.at[2], mid_recv.at[2], in_quad(1))

    part[...] = mine[...].astype(BF16)
    go(core_copy())
    core_copy().wait_recv()
    mine[...] = mine[...] + core_in[...].astype(F32)
    chip_out[...] = mine[pl.ds(pl.multiple_of(core * some, some), some), :].astype(BF16)
    go(chip_copy())
    chip_copy().wait_recv()
    go(half_copy(core))
    half_copy(1 - core).wait_recv()
    total = mine[...] + chip_in[...].astype(F32)
    gate_pre, up_pre, hidden_grad = (total[:, i * hw:(i + 1) * hw] for i in range(3))
    sigmoid_gate = 1.0 / (1.0 + jnp.exp(-gate_pre))
    activated = gate_pre * sigmoid_gate
    slope = up_pre * sigmoid_gate * (1.0 + gate_pre * (1.0 - sigmoid_gate))
    hid[:, 0:hw] = (hidden_grad * slope).astype(BF16)
    hid[:, hw:2 * hw] = (hidden_grad * activated).astype(BF16)
    hid[:, 2 * hw:3 * hw] = (activated * up_pre).astype(BF16)
    deltas = hid[:, 0:2 * hw]
    back[...] = dot(deltas, wgu[...], LAST)

    pieces = pieces_of(half)

    def rs_copy(way, i, p):
        route = rs_routes[way]
        _, at, width = pieces[p]
        span = pl.ds(at, width)
        src = summed.at[way, i + 1, :, span] if route.children(i) else leaf(way, i).at[:, span]
        k = i - route.parent(i)
        return copy(
            src, summed.at[way, i, :, span], rs_send.at[way, i - 1, p], rs_recv.at[way, i - 1, p],
            quad_at(-k if way == 0 else k),
        )

    def leaf(way, i):
        return leaves.at[way, 0 if i == rs_routes[way].far else 1]

    def own_block(way, i, span):
        at = place_of(way, i) * ROWS
        return back[at:at + ROWS, span]

    for step in range(to_right):
        for chain in range(2):
            for p, (_, at, width) in enumerate(pieces):
                span = slice(at, at + width)
                for way in range(2):
                    route = rs_routes[way]
                    i = (route.jump - 1 if chain else route.far) - step
                    if i < (1 if chain else max(route.jump, 1)):
                        continue
                    own = own_block(way, i, span)
                    if step == 0:
                        leaves[way, chain, :, span] = own.astype(BF16)
                    else:
                        rs_copy(way, i + 1, p).wait_recv()
                        summed[way, i + 1, :, span] = (
                            summed[way, i + 1, :, span].astype(F32) + own
                        ).astype(BF16)
                    go(rs_copy(way, i, p))

    def rel_copy(h, k, slot):
        return copy(
            relay.at[h], allrelay.at[h, slot], rel_send.at[h, k], rel_recv.at[h, k],
            (node_to(k), me_l),
        )

    for p, (h, at, width) in enumerate(pieces):
        span = slice(at, at + width)
        acc = back[0:ROWS, span]
        for way in (1, 0):
            for i in rs_routes[way].children(0):
                rs_copy(way, i, p).wait_recv()
                acc = acc + summed[way, i, :, span].astype(F32)
        relay[h, :, at - h * half:at - h * half + width] = acc.astype(BF16)
        if at + width == (h + 1) * half:
            for k in peers:
                go(rel_copy(h, k, me_n))

    allrelay[0, me_n] = relay[0]
    allrelay[1, me_n] = relay[1]
    grads = dot(xs[...], deltas, FIRST)
    gg_ref[...] = grads[:, :hw].astype(BF16)
    gu_ref[...] = grads[:, hw:].astype(BF16)
    gd_ref[...] = dot(hid[:, 2 * hw:3 * hw], dys[...], FIRST).astype(BF16)

    sums = jnp.zeros((cols, half), F32)
    for h in range(2):
        for k in peers:
            rel_copy(h, k, node_from(k)).wait_recv()
        sums = sums + dot(collect[h], allrelay[h].reshape(slots, half))
    fin_out[...] = sums.astype(BF16).reshape(DQ, 2 * TOK, half)

    def fin_copy(d, slot):
        return copy(
            fin_out.at[mate(d)], fin.at[slot], fin_send.at[d], fin_recv.at[d], in_quad(d)
        )

    for d in mates:
        go(fin_copy(d, b))
    fin[b] = fin_out[b]
    for d in mates:
        fin_copy(d, mate(d)).wait_recv()
    for c in started:
        c.wait_send()


def hand_on(fin, gg, gu, gd, gi_ref, gg_ref, gu_ref, gd_ref, gg_mid, gu_mid, gd_mid, sem):
    moves = ((gg, gg_mid, gg_ref), (gu, gu_mid, gu_ref), (gd, gd_mid, gd_ref))
    loads = [pltpu.make_async_copy(m[0], m[1], sem.at[0, i]) for i, m in enumerate(moves)]
    stores = [pltpu.make_async_copy(m[1], m[2], sem.at[1, i]) for i, m in enumerate(moves)]
    for c in loads:
        c.start()
    half = fin.shape[2]
    for q in range(DQ):
        got = fin[q].astype(F32)
        for h in range(2):
            at = (2 * q + h) * half
            gi_ref[:, at:at + half] = got[h * TOK:(h + 1) * TOK].astype(BF16)
    for load, store in zip(loads, stores):
        load.wait()
        store.start()
    for c in stores:
        c.wait()


def on_device(shape, grad_out, inputs, group_ids, pair_code, combine, w_gate, w_up, w_down):
    nodes, locals_ = shape
    nx = math.isqrt(nodes)
    ny = nodes // nx
    nq = locals_ // DQ
    feat, hw = w_gate.shape[1:]
    half = feat // 2
    width = grad_out.shape[1]
    ring = nq * ROWS
    slots = nodes * ROWS
    to_right = nq // 2
    pieces = len(pieces_of(half))
    dma = pltpu.SemaphoreType.DMA
    peers = nodes - 1
    operands = (
        grad_out, inputs, group_ids.T, pair_code.T, combine, w_gate[0], w_up[0], w_down[0]
    )
    outs = ((DQ, 2 * TOK, half), (feat, hw), (feat, hw), (hw, feat))

    def whole(dims):
        return pl.BlockSpec(dims, lambda i: (0,) * len(dims))

    hbm = pl.BlockSpec(memory_space=pl.ANY)
    results = pl.pallas_call(
        functools.partial(kernel, nx, ny, nq),
        grid=(1,),
        out_shape=tuple(jax.ShapeDtypeStruct(dims, BF16) for dims in outs),
        in_specs=[whole(o.shape) for o in operands],
        out_specs=tuple(whole(dims) for dims in outs),
        scratch_shapes=[
            pltpu.VMEM((2, DQ, 2 * TOK, half), BF16),
            pltpu.VMEM((2, DQ, 2 * TOK, half), BF16),
            pltpu.VMEM((GROUPS, LANES), F32),
            pltpu.VMEM((DQ, GROUPS, LANES), F32),
            pltpu.VMEM((4, nodes, ROWS, half), BF16),
            pltpu.VMEM((GROUPS, slots), BF16),
            pltpu.VMEM((nodes, GROUPS, slots), BF16),
            pltpu.VMEM((4, nx, nx, ROWS, half), BF16),
            pltpu.VMEM((4, nx, ROWS, half), BF16),
            pltpu.VMEM((4, nx, ROWS, half), BF16),
            pltpu.VMEM((ring, feat), BF16),
            pltpu.VMEM((ring, feat), BF16),
            pltpu.VMEM((feat, 2 * hw), BF16),
            pltpu.VMEM((ring, 3 * hw), F32),
            pltpu.VMEM((ring, 3 * hw), BF16),
            pltpu.VMEM((ring, 3 * hw), BF16),
            pltpu.VMEM((ring // 2, 3 * hw), BF16),
            pltpu.VMEM((ring, 3 * hw), BF16),
            pltpu.VMEM((ring, 3 * hw), BF16),
            pltpu.VMEM((ring, feat), F32),
            pltpu.VMEM((2, to_right + 1, ROWS, feat), BF16),
            pltpu.VMEM((2, 2, ROWS, feat), BF16),
            pltpu.VMEM((2, ROWS, half), BF16),
            pltpu.VMEM((2, nodes, ROWS, half), BF16),
            pltpu.VMEM((DQ, 2 * TOK, half), BF16),
            dma((2, DQ)), dma((2, DQ)), dma((DQ,)), dma((DQ,)),
            dma((4, nx)), dma((4, nx)), dma((4, nx)), dma((4, nx)),
            dma((peers,)), dma((peers,)),
            dma((4, nq)), dma((4, nq)),
            dma((3,)), dma((3,)),
            dma((2, to_right, pieces)), dma((2, to_right, pieces)),
            dma((2, peers)), dma((2, peers)), dma((DQ,)), dma((DQ,)),
        ],
        compiler_params=pltpu.CompilerParams(
            collective_id=0, has_side_effects=True, vmem_limit_bytes=56 * 1024 * 1024
        ),
    )(*operands)
    gi, gg, gu, gd = pl.pallas_call(
        hand_on,
        grid=(1,),
        out_shape=tuple(
            jax.ShapeDtypeStruct(dims, BF16) for dims in ((TOK, width),) + outs[1:]
        ),
        in_specs=[whole(outs[0]), hbm, hbm, hbm],
        out_specs=(whole((TOK, width)), hbm, hbm, hbm),
        scratch_shapes=[pltpu.VMEM(dims, BF16) for dims in outs[1:]] + [dma((2, 3))],
        compiler_params=pltpu.CompilerParams(vmem_limit_bytes=56 * 1024 * 1024),
    )(*results)
    return gi, gg[None], gu[None], gd[None]


def solution(mesh):
    rows = P(("node", "local"), None)
    blocks = P(("node", "local"), None, None)
    shape = (mesh.shape["node"], mesh.shape["local"])
    return jax.shard_map(
        functools.partial(on_device, shape),
        mesh=mesh,
        in_specs=(rows,) * 5 + (blocks,) * 3,
        out_specs=(rows,) + (blocks,) * 3,
        check_vma=False,
    )
```

```python
import functools
import math

import jax
import jax.numpy as jnp
from jax import lax
from jax.experimental import pallas as pl
from jax.experimental.pallas import tpu as pltpu
from jax.sharding import PartitionSpec as P

EXP_GROUP = 16
DQ = 4
CAPE = 4
TOK = 8
ROWS = DQ * CAPE
LANES = 128
GROUPS = 16
START = (0, 0, 0, 0)
AG_JUMP = (0, 0, 0, 0)
SPLIT = 1
RS_JUMP = 3
MESH = pl.DeviceIdType.MESH
F32 = jnp.float32
BF16 = jnp.bfloat16


def iota(shape, dim):
    return lax.broadcasted_iota(jnp.int32, shape, dim)


def grid_of(rows, cols):
    return iota((rows, cols), 0), iota((rows, cols), 1)


def one(where):
    return jnp.where(where, 1.0, 0.0).astype(BF16)


def dot(a, b, contract=((1,), (0,))):
    return lax.dot_general(a, b, (contract, ((), ())), preferred_element_type=F32)


LAST = ((1,), (1,))
FIRST = ((0,), (0,))


class Route:
    def __init__(self, far, jump):
        self.far = far
        self.jump = jump if 1 < jump <= far else 0

    def parent(self, i):
        return 0 if i == self.jump else i - 1

    def children(self, p):
        return [i for i in range(1, self.far + 1) if self.parent(i) == p]

    def arrival(self, i):
        return i if not self.jump or i < self.jump else i - self.jump + 2

    def last(self):
        return max(self.arrival(i) for i in range(1, self.far + 1))


def pieces_of(half):
    tiles = half // LANES
    lead = (tiles + 1) // 2 if SPLIT else tiles
    out = []
    for h in range(2):
        out.append((h, h * half, lead * LANES))
        if tiles > lead:
            out.append((h, h * half + lead * LANES, (tiles - lead) * LANES))
    return out


def kernel(
    nx, ny, nq,
    grad_ref, inp_ref, gid_ref, code_ref, comb_ref, wg_ref, wu_ref, wd_ref,
    fin, gg_out, gu_out, gd_out,
    gg_ref, gu_ref, gd_ref, wd_in, own_sem, tok_out, tok, win, wts, packed, cnt, cnts, arrived, turned, landed, xs, dys, wgu,
    mine, part, core_in, chip_out, chip_in, hid, back,
    summed, leaves, relay, allrelay, fin_out,
    tok_send, tok_recv, win_send, win_recv, along_send, along_recv, across_send, across_recv, cnt_send, cnt_recv,
    ag_send, ag_recv, mid_send, mid_recv,
    rs_send, rs_recv, rel_send, rel_recv, fin_send, fin_recv,
):
    nodes = nx * ny
    feat, hw = wg_ref.shape
    half = feat // 2
    slots = nodes * ROWS
    to_right = nq // 2
    steps_of = (to_right, nq - 1 - to_right)
    me_n = lax.axis_index("node")
    me_l = lax.axis_index("local")
    quad = lax.div(me_l, DQ)
    b = lax.rem(me_l, DQ)
    my_x, my_y = lax.div(me_n, ny), lax.rem(me_n, ny)

    def quad_at(k):
        return (me_n, lax.rem(quad + (k + nq) % nq, nq) * DQ + b)

    ag_routes = [[Route(far, jump) for far in steps_of] for jump in AG_JUMP]
    rs_routes = [Route(far, RS_JUMP) for far in steps_of]
    apart = {1, nq - 1}
    for route in sum(ag_routes, rs_routes):
        if route.jump:
            apart |= {route.jump, nq - route.jump}
    offsets = [(dx, dy) for dx in range(nx) for dy in range(ny) if dx or dy]
    peers = range(len(offsets))
    mates = range(1, DQ)
    spans = [pl.ds(h * half, half) for h in range(2)]
    started = []

    def go(c):
        c.start()
        started.append(c)

    def node_at(dx, dy):
        return lax.rem(my_x + dx, nx) * ny + lax.rem(my_y + dy, ny)

    def node_to(k):
        dx, dy = offsets[k]
        return node_at(dx, dy)

    def node_from(k):
        dx, dy = offsets[k]
        return node_at(nx - dx, ny - dy)

    def mate(d):
        return lax.bitwise_xor(b, d)

    def in_quad(d):
        return (me_n, quad * DQ + mate(d))

    def copy(src, dst, send, recv, device):
        return pltpu.make_async_remote_copy(
            src_ref=src, dst_ref=dst, send_sem=send, recv_sem=recv,
            device_id=device, device_id_type=MESH,
        )

    barrier = pltpu.get_barrier_semaphore()
    greet = [(node_to(k), me_l) for k in peers] + [in_quad(d) for d in mates]
    greet += [quad_at(k) for k in sorted(apart)]
    for device in greet:
        pl.semaphore_signal(barrier, inc=1, device_id=device, device_id_type=MESH)

    loads = [
        pltpu.make_async_copy(wg_ref, wgu.at[:, pl.ds(0, hw)], own_sem.at[0]),
        pltpu.make_async_copy(wu_ref, wgu.at[:, pl.ds(hw, hw)], own_sem.at[1]),
        pltpu.make_async_copy(wd_ref, wd_in, own_sem.at[2]),
    ]
    for c in loads:
        c.start()

    for q in range(DQ):
        for h in range(2):
            at = slice(q * feat + h * half, q * feat + (h + 1) * half)
            tok_out[h, q] = jnp.concatenate(
                [inp_ref[:, at].astype(F32), grad_ref[:, at].astype(F32)], axis=0
            ).astype(BF16)
    chosen, top = gid_ref.shape[0], comb_ref.shape[1]
    code = code_ref[...]
    first = jnp.zeros_like(code)
    for m in range(1, EXP_GROUP):
        first = first + jnp.where(code >= m * (EXP_GROUP - 1), 1, 0)
    second = first + 1 + (code - (EXP_GROUP - 1) * first)
    second = jnp.where(second >= EXP_GROUP, second - EXP_GROUP, second)
    row, col = grid_of(chosen, top)
    comb = comb_ref[...]
    weight = jnp.where(first == 0, dot(one(col == 2 * row), comb, LAST), 0.0)
    weight = weight + jnp.where(second == 0, dot(one(col == 2 * row + 1), comb, LAST), 0.0)
    window = jnp.zeros((GROUPS, TOK), F32)
    for k in range(chosen):
        named = iota((GROUPS, TOK), 0) == gid_ref[k:k + 1, :]
        window = window + jnp.where(named, weight[k:k + 1, :], 0.0)
    row, col = grid_of(TOK, LANES)
    win[...] = dot(window.astype(BF16), one(row == col))

    pl.semaphore_wait(barrier, len(greet))

    def tok_copy(d, h, slot):
        return copy(
            tok_out.at[h, mate(d)], tok.at[h, slot], tok_send.at[h, d], tok_recv.at[h, d],
            in_quad(d),
        )

    def win_copy(d, slot):
        return copy(win, wts.at[slot], win_send.at[d], win_recv.at[d], in_quad(d))

    for d in mates:
        go(win_copy(d, b))
    for h in range(2):
        for d in mates:
            go(tok_copy(d, h, b))
        tok[h, b] = tok_out[h, b]
    wts[b] = win[...]

    cols = 2 * DQ * TOK
    row, col = grid_of(cols, cols)
    below = one((row >> 3 == col >> 3) & (row < col))
    row, col = grid_of(cols, slots)
    tally = one((((row >> 3) & 1) == 0) & (row >> 4 == (col >> 2) & 3) & (col >> 4 == me_n))
    fold = nx.bit_length() - 1

    def group_at(order, u):
        return u if order == 0 else ((u & (nx - 1)) << fold) + (u >> fold)

    row, col = grid_of(slots, GROUPS)
    of_group = [one(group_at(order, row >> 4) == col) for order in range(2)]
    row, col = grid_of(GROUPS, slots)
    group_of = one(row == col >> 4)
    row, col = grid_of(slots, slots)
    before = one((row >> 4 < col >> 4) & ((row & 15) == (col & 15)))
    row, col = grid_of(slots, cols)
    own_base = one((row >> 4 == me_n) & ((row & 3) == 0) & (((row >> 2) & 3) == col >> 4))

    for d in mates:
        win_copy(d, mate(d)).wait_recv()
    weights = jnp.zeros((GROUPS, cols), F32)
    row, col = grid_of(LANES, cols)
    for j in range(DQ):
        weights = weights + dot(wts[j].astype(BF16), one((row == (col & 7)) & (col >> 4 == j)))
    live = one(weights > 0)
    ranks = dot(live, below)
    cnt[...] = dot(live, tally).astype(BF16)

    def cnt_copy(k, slot):
        return copy(cnt, cnts.at[slot], cnt_send.at[k], cnt_recv.at[k], (node_to(k), me_l))

    at_xy = (my_x, my_y)

    def node_on(axis, t):
        return t * ny + my_y if axis == 0 else my_x * ny + t

    def along_copy(c, k, slot):
        axis = c % 2
        t = lax.rem(at_xy[axis] + k, nx)
        return copy(
            packed.at[c, pl.ds(t * nx, nx)], arrived.at[c, slot],
            along_send.at[c, k], along_recv.at[c, k], (node_on(axis, t), me_l),
        )

    def across_copy(c, k, slot):
        axis = 1 - c % 2
        t = lax.rem(at_xy[axis] + k, nx)
        return copy(
            turned.at[c, t], landed.at[c, slot],
            across_send.at[c, k], across_recv.at[c, k], (node_on(axis, t), me_l),
        )

    picks = []
    row, col = grid_of(slots, cols)
    is_grad = ((col >> 3) & 1) == 1
    for order in range(2):
        w_at = dot(of_group[order], weights.astype(BF16))
        r_at = dot(of_group[order], ranks.astype(BF16))
        fits = ((row >> 2) & 3) == col >> 4
        fits = fits & (r_at == (row & 3).astype(F32)) & (w_at > 0)
        picks.append((
            one(fits & jnp.logical_not(is_grad)),
            jnp.where(fits & is_grad, w_at, 0.0).astype(BF16),
        ))

    def pack(c):
        a, h = c // 2, c % 2
        mine_at = at_xy[c % 2]
        rows = dot(picks[c % 2][a], tok[h].reshape(cols, half))
        packed[c] = rows.astype(BF16).reshape(nodes, ROWS, half)
        for k in range(1, nx):
            go(along_copy(c, k, mine_at))
        arrived[c, mine_at] = packed[c, pl.ds(mine_at * nx, nx)]

    for d in mates:
        tok_copy(d, 0, mate(d)).wait_recv()
    pack(0)
    for k in peers:
        go(cnt_copy(k, me_n))
    cnts[me_n] = cnt[...]
    for d in mates:
        tok_copy(d, 1, mate(d)).wait_recv()
    for c in range(1, 4):
        pack(c)

    for k in peers:
        cnt_copy(k, node_from(k)).wait_recv()
    counts = jnp.zeros((GROUPS, slots), F32)
    for m in range(nodes):
        counts = counts + cnts[m].astype(F32)
    begin = dot(counts.astype(BF16), before).astype(BF16)
    line = nx * ROWS
    merges = []
    for order in range(2):
        row, col = grid_of(line, GROUPS)
        group = my_x * ny + (row >> 4) if order == 0 else (row >> 4) * ny + my_y
        start = dot(one(group == col), begin).astype(BF16)
        row, col = grid_of(slots, slots)
        source = node_on(order, col >> (4 + fold))
        start = dot(
            start,
            one((row >> 4 == source) & ((row & 3) == 0) & ((row >> 2) & 3 == (col >> 2) & 3)),
        )
        row, col = grid_of(line, slots)
        same = (row >> 4 == (col >> 4) & (nx - 1)) & ((row >> 2) & 3 == (col >> 2) & 3)
        merges.append(one(same & ((row & 3).astype(F32) == start + (col & 3).astype(F32))))
    place = jnp.where(weights > 0, ranks + dot(begin, own_base), 255.0)
    place = dot(place.astype(BF16), group_of, FIRST)
    row, col = grid_of(cols, slots)
    stands = (row >> 4 == (col >> 2) & 3) & (place == (col & 3).astype(F32))
    collect = [one(stands & (((row >> 3) & 1) == h)) for h in range(2)]

    def turn_off(c):
        axis = c % 2
        for k in range(1, nx):
            along_copy(c, k, lax.rem(at_xy[axis] + nx - k, nx)).wait_recv()
        rows = dot(merges[axis], arrived[c].reshape(slots, half))
        turned[c] = rows.astype(BF16).reshape(nx, ROWS, half)
        here = at_xy[1 - axis]
        for k in range(1, nx):
            go(across_copy(c, k, here))
        landed[c, here] = turned[c, here]

    def land(c):
        here = at_xy[1 - c % 2]
        for k in range(1, nx):
            across_copy(c, k, lax.rem(here + nx - k, nx)).wait_recv()
        total = landed[c, 0].astype(F32)
        for k in range(1, nx):
            total = total + landed[c, k].astype(F32)
        rings[c // 2][0:ROWS, (c % 2) * half:(c % 2 + 1) * half] = total.astype(BF16)

    for c in range(4):
        if START[c] == 0:
            turn_off(c)
    for c in loads:
        c.wait()

    rings = (xs, dys)

    def block(c, i):
        return rings[c // 2].at[pl.ds(i * ROWS, ROWS), spans[c % 2]]

    def place_of(way, i):
        return i if way == 0 else (nq - i) % nq

    def ag_copy(c, way, i):
        p = ag_routes[c][way].parent(i)
        src, dst = place_of(way, p), place_of(way, i)
        return copy(
            block(c, src), block(c, dst), ag_send.at[c, dst], ag_recv.at[c, dst],
            quad_at(i - p if way == 0 else p - i),
        )

    def ag_wait(c, way, i):
        dst = place_of(way, i)
        copy(
            block(c, dst), block(c, dst), ag_send.at[c, dst], ag_recv.at[c, dst], quad_at(1)
        ).wait_recv()

    whole = set()

    def after_chunk(c):
        span = slice((c % 2) * half, (c % 2 + 1) * half)
        if c // 2 == 0:
            total, at = dot(xs[:, span], wgu[span, :]), slice(0, 2 * hw)
        else:
            total, at = dot(dys[:, span], wd_in[:, span], LAST), slice(2 * hw, 3 * hw)
        if c ^ 1 in whole:
            total = mine[:, at] + total
        mine[:, at] = total
        whole.add(c)

    last = [max(route.last() for route in routes) for routes in ag_routes]
    for turn in range(max(last[c] + START[c] for c in range(4)) + 1):
        for c in range(4):
            step = turn - START[c]
            if step == 0:
                land(c)
                for way in range(2):
                    for i in reversed(ag_routes[c][way].children(0)):
                        go(ag_copy(c, way, i))
            for way in range(2):
                route = ag_routes[c][way]
                for i in range(route.far, 0, -1):
                    if route.arrival(i) == step:
                        ag_wait(c, way, i)
                        for j in route.children(i):
                            go(ag_copy(c, way, j))
            if step == last[c]:
                after_chunk(c)
        for c in range(4):
            if START[c] == turn + 1:
                turn_off(c)

    core = lax.bitwise_and(b, 1)
    some = nq * ROWS // 2

    def rows_of(ref, owner):
        return ref.at[pl.ds(pl.multiple_of(owner * some, some), some)]

    def core_copy():
        return copy(part, core_in, mid_send.at[0], mid_recv.at[0], in_quad(1))

    def chip_copy():
        return copy(chip_out, rows_of(chip_in, core), mid_send.at[1], mid_recv.at[1], in_quad(2))

    def half_copy(owner):
        rows = rows_of(chip_in, owner)
        return copy(rows, rows, mid_send.at[2], mid_recv.at[2], in_quad(1))

    part[...] = mine[...].astype(BF16)
    go(core_copy())
    core_copy().wait_recv()
    mine[...] = mine[...] + core_in[...].astype(F32)
    chip_out[...] = mine[pl.ds(pl.multiple_of(core * some, some), some), :].astype(BF16)
    go(chip_copy())
    chip_copy().wait_recv()
    go(half_copy(core))
    half_copy(1 - core).wait_recv()
    total = mine[...] + chip_in[...].astype(F32)
    gate_pre, up_pre, hidden_grad = (total[:, i * hw:(i + 1) * hw] for i in range(3))
    sigmoid_gate = 1.0 / (1.0 + jnp.exp(-gate_pre))
    activated = gate_pre * sigmoid_gate
    slope = up_pre * sigmoid_gate * (1.0 + gate_pre * (1.0 - sigmoid_gate))
    hid[:, 0:hw] = (hidden_grad * slope).astype(BF16)
    hid[:, hw:2 * hw] = (hidden_grad * activated).astype(BF16)
    hid[:, 2 * hw:3 * hw] = (activated * up_pre).astype(BF16)
    deltas = hid[:, 0:2 * hw]
    back[...] = dot(deltas, wgu[...], LAST)

    pieces = pieces_of(half)

    def rs_copy(way, i, p):
        route = rs_routes[way]
        _, at, width = pieces[p]
        span = pl.ds(at, width)
        src = summed.at[way, i + 1, :, span] if route.children(i) else leaf(way, i).at[:, span]
        k = i - route.parent(i)
        return copy(
            src, summed.at[way, i, :, span], rs_send.at[way, i - 1, p], rs_recv.at[way, i - 1, p],
            quad_at(-k if way == 0 else k),
        )

    def leaf(way, i):
        return leaves.at[way, 0 if i == rs_routes[way].far else 1]

    def own_block(way, i, span):
        at = place_of(way, i) * ROWS
        return back[at:at + ROWS, span]

    for step in range(to_right):
        for chain in range(2):
            for p, (_, at, width) in enumerate(pieces):
                span = slice(at, at + width)
                for way in range(2):
                    route = rs_routes[way]
                    i = (route.jump - 1 if chain else route.far) - step
                    if i < (1 if chain else max(route.jump, 1)):
                        continue
                    own = own_block(way, i, span)
                    if step == 0:
                        leaves[way, chain, :, span] = own.astype(BF16)
                    else:
                        rs_copy(way, i + 1, p).wait_recv()
                        summed[way, i + 1, :, span] = (
                            summed[way, i + 1, :, span].astype(F32) + own
                        ).astype(BF16)
                    go(rs_copy(way, i, p))

    def rel_copy(h, k, slot):
        return copy(
            relay.at[h], allrelay.at[h, slot], rel_send.at[h, k], rel_recv.at[h, k],
            (node_to(k), me_l),
        )

    for p, (h, at, width) in enumerate(pieces):
        span = slice(at, at + width)
        acc = back[0:ROWS, span]
        for way in (1, 0):
            for i in rs_routes[way].children(0):
                rs_copy(way, i, p).wait_recv()
                acc = acc + summed[way, i, :, span].astype(F32)
        relay[h, :, at - h * half:at - h * half + width] = acc.astype(BF16)
        if at + width == (h + 1) * half:
            for k in peers:
                go(rel_copy(h, k, me_n))

    allrelay[0, me_n] = relay[0]
    allrelay[1, me_n] = relay[1]
    grads = dot(xs[...], deltas, FIRST)
    gg_ref[...] = grads[:, :hw].astype(BF16)
    gu_ref[...] = grads[:, hw:].astype(BF16)
    gd_ref[...] = dot(hid[:, 2 * hw:3 * hw], dys[...], FIRST).astype(BF16)
    stores = [
        pltpu.make_async_copy(gg_ref, gg_out, own_sem.at[3]),
        pltpu.make_async_copy(gu_ref, gu_out, own_sem.at[4]),
        pltpu.make_async_copy(gd_ref, gd_out, own_sem.at[5]),
    ]
    for c in stores:
        c.start()

    sums = jnp.zeros((cols, half), F32)
    for h in range(2):
        for k in peers:
            rel_copy(h, k, node_from(k)).wait_recv()
        sums = sums + dot(collect[h], allrelay[h].reshape(slots, half))
    fin_out[...] = sums.astype(BF16).reshape(DQ, 2 * TOK, half)

    def fin_copy(d, slot):
        return copy(
            fin_out.at[mate(d)], fin.at[slot], fin_send.at[d], fin_recv.at[d], in_quad(d)
        )

    for d in mates:
        go(fin_copy(d, b))
    fin[b] = fin_out[b]
    for d in mates:
        fin_copy(d, mate(d)).wait_recv()
    for c in stores:
        c.wait()
    for c in started:
        c.wait_send()


def hand_on(fin, gg, gu, gd, gi_ref, gg_ref, gu_ref, gd_ref, gg_mid, gu_mid, gd_mid, sem):
    moves = ((gg, gg_mid, gg_ref), (gu, gu_mid, gu_ref), (gd, gd_mid, gd_ref))
    loads = [pltpu.make_async_copy(m[0], m[1], sem.at[0, i]) for i, m in enumerate(moves)]
    stores = [pltpu.make_async_copy(m[1], m[2], sem.at[1, i]) for i, m in enumerate(moves)]
    for c in loads:
        c.start()
    half = fin.shape[2]
    for q in range(DQ):
        got = fin[q].astype(F32)
        for h in range(2):
            at = (2 * q + h) * half
            gi_ref[:, at:at + half] = got[h * TOK:(h + 1) * TOK].astype(BF16)
    for load, store in zip(loads, stores):
        load.wait()
        store.start()
    for c in stores:
        c.wait()


def on_device(shape, grad_out, inputs, group_ids, pair_code, combine, w_gate, w_up, w_down):
    nodes, locals_ = shape
    nx = math.isqrt(nodes)
    ny = nodes // nx
    nq = locals_ // DQ
    feat, hw = w_gate.shape[1:]
    half = feat // 2
    width = grad_out.shape[1]
    ring = nq * ROWS
    slots = nodes * ROWS
    to_right = nq // 2
    pieces = len(pieces_of(half))
    dma = pltpu.SemaphoreType.DMA
    peers = nodes - 1
    operands = (
        grad_out, inputs, group_ids.T, pair_code.T, combine, w_gate[0], w_up[0], w_down[0]
    )
    outs = ((DQ, 2 * TOK, half), (feat, hw), (feat, hw), (hw, feat))

    def whole(dims):
        return pl.BlockSpec(dims, lambda i: (0,) * len(dims))

    hbm = pl.BlockSpec(memory_space=pl.ANY)
    results = pl.pallas_call(
        functools.partial(kernel, nx, ny, nq),
        grid=(1,),
        out_shape=tuple(jax.ShapeDtypeStruct(dims, BF16) for dims in outs),
        in_specs=[whole(o.shape) for o in operands[:5]] + [hbm] * 3,
        out_specs=(whole(outs[0]), hbm, hbm, hbm),
        scratch_shapes=[pltpu.VMEM(dims, BF16) for dims in outs[1:] + outs[3:]] + [
            dma((6,)),
            pltpu.VMEM((2, DQ, 2 * TOK, half), BF16),
            pltpu.VMEM((2, DQ, 2 * TOK, half), BF16),
            pltpu.VMEM((GROUPS, LANES), F32),
            pltpu.VMEM((DQ, GROUPS, LANES), F32),
            pltpu.VMEM((4, nodes, ROWS, half), BF16),
            pltpu.VMEM((GROUPS, slots), BF16),
            pltpu.VMEM((nodes, GROUPS, slots), BF16),
            pltpu.VMEM((4, nx, nx, ROWS, half), BF16),
            pltpu.VMEM((4, nx, ROWS, half), BF16),
            pltpu.VMEM((4, nx, ROWS, half), BF16),
            pltpu.VMEM((ring, feat), BF16),
            pltpu.VMEM((ring, feat), BF16),
            pltpu.VMEM((feat, 2 * hw), BF16),
            pltpu.VMEM((ring, 3 * hw), F32),
            pltpu.VMEM((ring, 3 * hw), BF16),
            pltpu.VMEM((ring, 3 * hw), BF16),
            pltpu.VMEM((ring // 2, 3 * hw), BF16),
            pltpu.VMEM((ring, 3 * hw), BF16),
            pltpu.VMEM((ring, 3 * hw), BF16),
            pltpu.VMEM((ring, feat), F32),
            pltpu.VMEM((2, to_right + 1, ROWS, feat), BF16),
            pltpu.VMEM((2, 2, ROWS, feat), BF16),
            pltpu.VMEM((2, ROWS, half), BF16),
            pltpu.VMEM((2, nodes, ROWS, half), BF16),
            pltpu.VMEM((DQ, 2 * TOK, half), BF16),
            dma((2, DQ)), dma((2, DQ)), dma((DQ,)), dma((DQ,)),
            dma((4, nx)), dma((4, nx)), dma((4, nx)), dma((4, nx)),
            dma((peers,)), dma((peers,)),
            dma((4, nq)), dma((4, nq)),
            dma((3,)), dma((3,)),
            dma((2, to_right, pieces)), dma((2, to_right, pieces)),
            dma((2, peers)), dma((2, peers)), dma((DQ,)), dma((DQ,)),
        ],
        compiler_params=pltpu.CompilerParams(
            collective_id=0, has_side_effects=True, vmem_limit_bytes=56 * 1024 * 1024
        ),
    )(*operands)
    gi, gg, gu, gd = pl.pallas_call(
        hand_on,
        grid=(1,),
        out_shape=tuple(
            jax.ShapeDtypeStruct(dims, BF16) for dims in ((TOK, width),) + outs[1:]
        ),
        in_specs=[whole(outs[0]), hbm, hbm, hbm],
        out_specs=(whole((TOK, width)), hbm, hbm, hbm),
        scratch_shapes=[pltpu.VMEM(dims, BF16) for dims in outs[1:]] + [dma((2, 3))],
        compiler_params=pltpu.CompilerParams(vmem_limit_bytes=56 * 1024 * 1024),
    )(*results)
    return gi, gg[None], gu[None], gd[None]


def solution(mesh):
    rows = P(("node", "local"), None)
    blocks = P(("node", "local"), None, None)
    shape = (mesh.shape["node"], mesh.shape["local"])
    return jax.shard_map(
        functools.partial(on_device, shape),
        mesh=mesh,
        in_specs=(rows,) * 5 + (blocks,) * 3,
        out_specs=(rows,) + (blocks,) * 3,
        check_vma=False,
    )
```
